32 devices in a mesh: dp: 8 (over y, x, core), fsdp: 4 (over z).
Axes of the slice: x: 2, y: 2, z: 4, core: 2. Of those that a mesh axis runs over, the one named last changes fastest.
Arguments:
- patches: bfloat16 [32, 8, 196, 768], P(('dp', 'fsdp')), may hold values from -6 to 6
- class_token: bfloat16 [32, 768], P(('dp', 'fsdp')), may hold values from -6 to 6
- keep_mask: int32 [32, 8, 196], P(('dp', 'fsdp')), may hold values from 0 to 1, as said below
- time_gain: bfloat16 [768], P(('dp', 'fsdp')), may hold values from 0.5 to 1.5
- time_bias: bfloat16 [768], P(('dp', 'fsdp')), may hold values from -3 to 3
- time_project: bfloat16 [768, 2304], P(('dp', 'fsdp')), may hold values from -0.21875 to 0.21875
- time_output: bfloat16 [768, 768], P(('dp', 'fsdp')), may hold values from -0.4375 to 0.4375
- time_mixer: bfloat16 [768, 768], P(('dp', 'fsdp')), may hold values from -0.21875 to 0.21875
- space_gain: bfloat16 [768], P(('dp', 'fsdp')), may hold values from 0.5 to 1.5
- space_bias: bfloat16 [768], P(('dp', 'fsdp')), may hold values from -3 to 3
- space_project: bfloat16 [768, 2304], P(('dp', 'fsdp')), may hold values from -0.21875 to 0.21875
- space_output: bfloat16 [768, 768], P(('dp', 'fsdp')), may hold values from -1.75 to 1.75
- dense_gain: bfloat16 [768], P(('dp', 'fsdp')), may hold values from 0.5 to 1.5
- dense_bias: bfloat16 [768], P(('dp', 'fsdp')), may hold values from -3 to 3
- dense_in: bfloat16 [768, 3072], P(('dp', 'fsdp')), may hold values from -0.21875 to 0.21875
- dense_out: bfloat16 [3072, 768], P(('dp', 'fsdp')), may hold values from -0.109375 to 0.109375
- cotangent_patches: bfloat16 [32, 8, 196, 768], P(('dp', 'fsdp')), may hold values from -6 to 6
- cotangent_class: bfloat16 [32, 768], P(('dp', 'fsdp')), may hold values from -6 to 6
Outputs:
- patches_out: bfloat16 [32, 8, 196, 768], P(('dp', 'fsdp'))
- class_out: bfloat16 [32, 768], P(('dp', 'fsdp'))
- grad_patches: bfloat16 [32, 8, 196, 768], P(('dp', 'fsdp'))
- grad_class: bfloat16 [32, 768], P(('dp', 'fsdp'))
- grad_time_gain: float32 [768], P(('dp', 'fsdp'))
- grad_time_bias: float32 [768], P(('dp', 'fsdp'))
- grad_time_project: float32 [768, 2304], P(('dp', 'fsdp'))
- grad_time_output: float32 [768, 768], P(('dp', 'fsdp'))
- grad_time_mixer: float32 [768, 768], P(('dp', 'fsdp'))
- grad_space_gain: float32 [768], P(('dp', 'fsdp'))
- grad_space_bias: float32 [768], P(('dp', 'fsdp'))
- grad_space_project: float32 [768, 2304], P(('dp', 'fsdp'))
- grad_space_output: float32 [768, 768], P(('dp', 'fsdp'))
- grad_dense_gain: float32 [768], P(('dp', 'fsdp'))
- grad_dense_bias: float32 [768], P(('dp', 'fsdp'))
- grad_dense_in: float32 [768, 3072], P(('dp', 'fsdp'))
- grad_dense_out: float32 [3072, 768], P(('dp', 'fsdp'))
The draws below stay inside these ranges and needn't reach their ends.
Inputs may be any that keep to these rules, and one draw needn't show every extreme that they name: `keep_mask`: 1 keeps a patch of a frame, 0 drops it.
All inputs are finite; a program needn't handle non-finite values.
Results may differ from the reference program's by a relative error of at most 0.019.
Values may be sent and summed in bfloat16 or wider, within the bound.
A program may use at most 320 MiB of HBM per device.

```python
import jax
import jax.numpy as jnp
from jax import lax

D = 768
FF = 3072
HEADS = 12
HEAD = 64
FRAMES = 8
PATCH = 196
CLIPS = 32


def draw_keep_mask(key, part):
    key = jax.random.fold_in(key, 7)
    level_key, flip_key = jax.random.split(key)
    levels = jax.random.randint(level_key, (CLIPS, 1, 1), 2, 9)
    coin_flips = jax.random.randint(flip_key, (CLIPS, FRAMES, PATCH), 0, 8)
    return (coin_flips < levels).astype(jnp.int32)


def level_of(rng, dims, cuts, low, largest):
    loudness = 1.0
    for axis_at, blocks in cuts:
        heights = jax.random.uniform(jax.random.fold_in(jax.random.fold_in(rng, 6), axis_at), (blocks,), jnp.float32, low / len(cuts), largest / len(cuts))
        loudness = loudness * jnp.repeat(jnp.exp(heights), dims[axis_at] // blocks).reshape((-1,) + (1,) * (len(dims) - 1 - axis_at))
    return loudness


def centred(own_key, shape, scale, limit, cuts=(), kind=jnp.bfloat16):
    array = scale * jax.random.normal(own_key, shape, jnp.float32)
    if cuts:
        array = array * level_of(own_key, shape, cuts, -0.22, 0.18)
    return jnp.clip(array, -limit, limit).astype(kind)


def setup_inputs(seed: int = 0) -> dict:
    keys = jax.random.split(jax.random.key(seed), 19)
    patches = centred(keys[0], (CLIPS, FRAMES, PATCH, D), 1.0, 6.0, ((0, 32),))
    class_token = centred(keys[1], (CLIPS, D), 1.0, 6.0, ((0, 32),))
    keep_mask = draw_keep_mask(jax.random.fold_in(keys[18], 71), 0)
    time_gain = jnp.clip(1.0 + 0.1 * jax.random.normal(keys[3], (D,), jnp.float32), 0.5, 1.5).astype(jnp.bfloat16)
    time_bias = centred(keys[4], (D,), 0.3, 3.0, ((0, 32),))
    time_project = centred(keys[5], (D, 3 * D), D ** -0.5, 0.21875, ((0, 32),))
    time_output = centred(keys[6], (D, D), (2 * D // FRAMES) ** -0.5, 0.4375, ((0, 32),))
    time_mixer = centred(keys[7], (D, D), D ** -0.5, 0.21875, ((0, 32),))
    space_gain = jnp.clip(1.0 + 0.1 * jax.random.normal(keys[8], (D,), jnp.float32), 0.5, 1.5).astype(jnp.bfloat16)
    space_bias = centred(keys[9], (D,), 0.3, 3.0, ((0, 32),))
    space_project = centred(keys[10], (D, 3 * D), D ** -0.5, 0.21875, ((0, 32),))
    space_output = centred(keys[11], (D, D), (max(1, 3 * D // (PATCH + 1))) ** -0.5, 1.75, ((0, 32),))
    dense_gain = jnp.clip(1.0 + 0.1 * jax.random.normal(keys[12], (D,), jnp.float32), 0.5, 1.5).astype(jnp.bfloat16)
    dense_bias = centred(keys[13], (D,), 0.3, 3.0, ((0, 32),))
    dense_in = centred(keys[14], (D, FF), D ** -0.5, 0.21875, ((0, 32),))
    dense_out = centred(keys[15], (FF, D), FF ** -0.5, 0.109375, ((0, 32),))
    cotangent_patches = centred(keys[16], (CLIPS, FRAMES, PATCH, D), 1.0, 6.0, ((0, 32),))
    cotangent_class = centred(keys[17], (CLIPS, D), 1.0, 6.0, ((0, 32),))
    return {"patches": patches, "class_token": class_token, "keep_mask": keep_mask, "time_gain": time_gain, "time_bias": time_bias, "time_project": time_project, "time_output": time_output, "time_mixer": time_mixer, "space_gain": space_gain, "space_bias": space_bias, "space_project": space_project, "space_output": space_output, "dense_gain": dense_gain, "dense_bias": dense_bias, "dense_in": dense_in, "dense_out": dense_out, "cotangent_patches": cotangent_patches, "cotangent_class": cotangent_class}


EPS = 1e-06
NEG = -1000000000.0
HIGH = lax.Precision.HIGHEST

@jax.custom_vjp
def low(v):
    return lax.optimization_barrier(v.astype(jnp.bfloat16)).astype(jnp.float32)

@jax.custom_vjp
def low_back(v):
    return v

def low_keep(v):
    return (low(v), None)

def low_pass(kept, grad):
    return (grad,)

def back_keep(v):
    return (v, None)

def back_low(kept, grad):
    return (low(grad),)
low.defvjp(low_keep, low_pass)
low_back.defvjp(back_keep, back_low)

def round_both(values):
    return low(low_back(values))

def norm_rows(values, gain_vec, offset):
    centre = values - lax.optimization_barrier(jnp.mean(values, axis=-1, keepdims=True))
    spread = lax.optimization_barrier(jnp.mean(centre * centre, axis=-1, keepdims=True))
    return centre * lax.rsqrt(spread + EPS) * gain_vec + offset

def matmul(operand, matrix):
    return jnp.einsum('...d,de->...e', operand, matrix, precision=HIGH)

def split_heads(packed):
    shape = packed.shape[:-1] + (HEADS, HEAD)
    return (packed[..., :D].reshape(shape), packed[..., D:2 * D].reshape(shape), packed[..., 2 * D:].reshape(shape))

def attend(queries, key_rows, values, allowed):
    scores = low_back(jnp.einsum('blhe,bmhe->bhlm', queries, key_rows, precision=HIGH))
    logits = jnp.where(allowed[:, None, None, :] > 0.5, scores * HEAD ** (-0.5), NEG)
    softmax_rows = low(jax.nn.softmax(logits, axis=-1))
    return jnp.einsum('bhlm,bmhe->blhe', softmax_rows, values, precision=HIGH)

def clip_forward(params, patch_rows, class_row, keep_rows):
    time_gain, time_bias, time_project, time_output, time_mixer, space_gain, space_bias, space_project, space_output, dense_gain, dense_bias, dense_in, dense_out = params
    time_normed = low(norm_rows(patch_rows, time_gain, time_bias))
    time_packed = round_both(matmul(time_normed, time_project))
    by_place = jnp.transpose(time_packed, (1, 0, 2))
    queries, key_rows, values = split_heads(by_place)
    time_mixed = attend(queries, key_rows, values, jnp.transpose(keep_rows))
    time_mixed = round_both(jnp.transpose(time_mixed.reshape(PATCH, FRAMES, D), (1, 0, 2)))
    time_projected = round_both(matmul(time_mixed, time_output))
    time_branch = low_back(matmul(time_projected, time_mixer))
    after_time = patch_rows + time_branch * keep_rows[:, :, None]
    frame_rows = jnp.concatenate([jnp.broadcast_to(class_row[None, None, :], (FRAMES, 1, D)), after_time], axis=1)
    space_normed = low(norm_rows(frame_rows, space_gain, space_bias))
    space_packed = round_both(matmul(space_normed, space_project))
    queries, key_rows, values = split_heads(space_packed)
    frame_allowed = jnp.concatenate([jnp.ones((FRAMES, 1), keep_rows.dtype), keep_rows], axis=1)
    space_mixed = round_both(attend(queries, key_rows, values, frame_allowed).reshape(FRAMES, PATCH + 1, D))
    space_branch = low_back(matmul(space_mixed, space_output))
    after_space = after_time + space_branch[:, 1:] * keep_rows[:, :, None]
    class_after = class_row + lax.optimization_barrier(jnp.mean(space_branch[:, 0], axis=0))
    token_rows = jnp.concatenate([class_after[None], after_space.reshape(FRAMES * PATCH, D)], axis=0)
    row_keep = jnp.concatenate([jnp.ones((1,), keep_rows.dtype), keep_rows.reshape(FRAMES * PATCH)])
    dense_normed = low(norm_rows(token_rows, dense_gain, dense_bias))
    hidden_pre = low_back(matmul(dense_normed, dense_in))
    hidden_act = low(jax.nn.gelu(hidden_pre, approximate=False))
    dense_branch = low_back(matmul(hidden_act, dense_out))
    result = token_rows + dense_branch * row_keep[:, None]
    return (result[1:].reshape(FRAMES, PATCH, D), result[0])

def reference(patches, class_token, keep_mask, time_gain, time_bias, time_project, time_output, time_mixer, space_gain, space_bias, space_project, space_output, dense_gain, dense_bias, dense_in, dense_out, cotangent_patches, cotangent_class):
    params = tuple((weight.astype(jnp.float32) for weight in (time_gain, time_bias, time_project, time_output, time_mixer, space_gain, space_bias, space_project, space_output, dense_gain, dense_bias, dense_in, dense_out)))
    keep_float = keep_mask.astype(jnp.float32)

    def per_clip(summed, clip_items):
        patch_rows, class_row, keep_rows, grad_rows, grad_row = clip_items

        def forward_clip(weights, inputs, class_in):
            return clip_forward(weights, inputs, class_in, keep_rows)
        outputs, pullback = jax.vjp(forward_clip, params, patch_rows, class_row)
        grad_params, grad_inputs, grad_class_in = pullback((grad_rows, grad_row))
        summed = jax.tree.map(lambda acc, term: acc + term, summed, grad_params)
        return (summed, (outputs[0].astype(jnp.bfloat16), outputs[1].astype(jnp.bfloat16), grad_inputs.astype(jnp.bfloat16), grad_class_in.astype(jnp.bfloat16)))
    blank_grads = tuple((jnp.zeros_like(weight) for weight in params))
    summed, stacked = lax.scan(per_clip, blank_grads, (patches.astype(jnp.float32), class_token.astype(jnp.float32), keep_float, cotangent_patches.astype(jnp.float32), cotangent_class.astype(jnp.float32)))
    return (stacked[0], stacked[1], stacked[2], stacked[3], summed[0], summed[1], summed[2], summed[3], summed[4], summed[5], summed[6], summed[7], summed[8], summed[9], summed[10], summed[11], summed[12])
```

```python
import functools

import jax
import jax.numpy as jnp
import numpy as np
from jax import lax
from jax.experimental import pallas as pl
from jax.experimental.pallas import tpu as pltpu
from jax.sharding import PartitionSpec as P

HEADS = 12
HEAD = 64
EPS = 1e-06
NEG = -1000000000.0
FAR = -1e30
PLACES = 14
AXES = ("dp", "fsdp")
BF = jnp.bfloat16
F32 = jnp.float32
LIMIT = 62 * 2**20

ERFC_P = 0.255
ERFC_C = (
    0.10110071301460266,
    0.11016720533370972,
    0.04771651700139046,
    0.2258773148059845,
    -0.18891476094722748,
    0.2874106466770172,
    -0.08335751295089722,
)
ROOT_2PI_INV = 0.3989422804014327

NT = (((1,), (1,)), ((), ()))
TN = (((0,), (0,)), ((), ()))
NN = (((1,), (0,)), ((), ()))


def dot(left, right, dims=NN):
    return lax.dot_general(left, right, dims, preferred_element_type=F32)


def gelu_pair(u):
    size = jnp.abs(u)
    den = 1.0 + ERFC_P * size
    t = pl.reciprocal(den, approx=True)
    t = t * (2.0 - den * t)
    bell = jnp.exp(-0.5 * u * u)
    poly = jnp.full_like(u, ERFC_C[-1])
    for coef in ERFC_C[-2::-1]:
        poly = poly * t + coef
    tail = poly * t * bell
    cdf = jnp.where(u < 0.0, tail, 1.0 - tail)
    return u * cdf, cdf + (ROOT_2PI_INV * u) * bell


def norm_stats(values):
    centre = values - jnp.mean(values, axis=-1, keepdims=True)
    spread = jnp.mean(centre * centre, axis=-1, keepdims=True)
    scale = lax.rsqrt(spread + EPS)
    return centre * scale, scale


def norm_back(xhat, scale, gain, grad):
    scaled = grad * gain
    first = jnp.mean(scaled, axis=-1, keepdims=True)
    second = jnp.mean(scaled * xhat, axis=-1, keepdims=True)
    return scale * (scaled - first - xhat * second)


def fold8(values):
    rows, width = values.shape
    return jnp.sum(values.reshape(rows // 8, 8, width), axis=0)


def lane_masks(scale):
    lane = lax.broadcasted_iota(jnp.int32, (1, 128), 1)
    low = jnp.where(lane < HEAD, scale, 0.0)
    return low.astype(BF), (scale - low).astype(BF)


def two_heads(values, masks):
    rest = jnp.zeros((-values.shape[0] % 128, 128), values.dtype)
    return jnp.concatenate([values * masks[0], rest, values * masks[1], rest], axis=0)


def pick_heads(both, rows):
    half = both.shape[1] // 2
    return jnp.concatenate([both[:HEAD, :half], both[HEAD:, half:]], axis=0).T[:rows]


def attend_unit(q, k, v, bias):
    scores = dot(k, two_heads(q, lane_masks(0.125)), NT) + bias
    peak = jnp.max(scores, axis=0, keepdims=True)
    raised = jnp.exp(scores - peak)
    probs = (raised * (1.0 / jnp.sum(raised, axis=0, keepdims=True))).astype(BF)
    return probs, pick_heads(dot(v.T, probs), q.shape[0]).astype(BF)


def attend_unit_back(q, k, v, probs, grad):
    grad_two = two_heads(grad, lane_masks(1.0))
    grad_probs = dot(v, grad_two, NT)
    wide = probs.astype(F32)
    inner = jnp.sum(wide * grad_probs, axis=0, keepdims=True)
    grad_scores = (wide * (grad_probs - inner)).astype(BF)
    grad_v = dot(probs, grad_two)
    grad_k = dot(grad_scores, two_heads(q, lane_masks(0.125)))
    grad_q = pick_heads(dot(k.T, grad_scores) * 0.125, q.shape[0])
    return grad_q.astype(BF), grad_k.astype(BF), grad_v.astype(BF)


MESH = pl.DeviceIdType.MESH
HOPS = 3


def place_of():
    dp, z = lax.axis_index("dp"), lax.axis_index("fsdp")
    return dp // 4, (dp // 2) % 2, dp % 2, z


def device_of(y, x, c, z):
    return ((y * 2 + x) * 2 + c, z)


def partners():
    y, x, c, z = place_of()
    return [device_of(y, x, c, (z + k) % 4) for k in range(1, 4)] + [
        device_of(1 - y, x, c, z), device_of(y, 1 - x, c, z), device_of(y, x, 1 - c, z)
    ]


def meet():
    barrier = pltpu.get_barrier_semaphore()
    others = partners()
    for other in others:
        pl.semaphore_signal(barrier, inc=1, device_id=other, device_id_type=MESH)
    pl.semaphore_wait(barrier, len(others))


def remote(src, dst, send, recv, slot, device):
    return pltpu.make_async_remote_copy(
        src_ref=src, dst_ref=dst, send_sem=send.at[slot], recv_sem=recv.at[slot],
        device_id=device, device_id_type=MESH,
    )


SLOTS = 6


class Spread:
    def __init__(self, src, dst, send, recv, slot, device, depth=3):
        self.whole = remote(src, dst, send, recv, slot, device)
        self.parts = [
            remote(src.at[at] if at else src, dst.at[at] if at else dst, send, recv, slot, device) for at in np.ndindex(*src.shape[:-depth])
        ]

    def start(self):
        for part in self.parts:
            part.start()

    def wait_recv(self):
        self.whole.wait_recv()

    def wait_send(self):
        self.whole.wait_send()


LINK = 0.09
PAIR = 0.4
HOP = 2.0
GATHER = ((("z", 8), ("x", 8), ("y", 16), ("c", 16)), (("z", 8), ("y", 8), ("x", 16), ("c", 16)))
SCATTER = ((("c", 16), ("y", 16), ("x", 8), ("z", 8)), (("c", 16), ("x", 16), ("y", 8), ("z", 8)))


def plan(chunks, starts):
    free, events, pending = {}, [], []
    first_ends = []

    def issue(now, chunk, phase):
        axes, units = chunks[chunk][0][phase]
        amount = units * chunks[chunk][1] * 1.024 / 1000.0
        end = now
        for axis in axes:
            low = max(now, free.get(axis, 0.0))
            free[axis] = low + amount / (PAIR if axis == "c" else LINK)
            end = max(end, free[axis])
        pending.append((end + HOP, chunk, phase + 1))

    waiting = [i for i, t in enumerate(starts) if t is None]
    for i in waiting[:2]:
        pending.append((0.0, i, 0))
    waiting = waiting[2:]
    pending += [(t, i, 0) for i, t in enumerate(starts) if t is not None]
    while pending:
        pending.sort()
        now, chunk, step = pending.pop(0)
        events.append((now, chunk, step))
        if step < 4:
            issue(now, chunk, step)
        if step == 1 and starts[chunk] is None and waiting:
            pending.append((now, waiting.pop(0), 0))
    return events


class Clock:
    def __init__(self, chunks=(), starts=None, pace=1.0):
        self.pace = pace
        self.steps = [c[2] for c in chunks]
        self.starts = starts or [None] * len(chunks)
        self.events = plan([c[:2] for c in chunks], self.starts)
        self.done = set()
        self.now = 0.0

    def run(self):
        now, chunk, step = self.events.pop(0)
        self.now = max(self.now, now)
        self.steps[chunk][step]()
        self.done.add((chunk, step))

    def spend(self, time):
        self.now += self.pace * time
        while self.events and self.events[0][0] <= self.now:
            self.run()

    def need(self, chunk, step=4):
        while self.steps and (chunk, step) not in self.done:
            self.run()

    def drain(self):
        while self.events:
            self.run()

    def close(self):
        for steps in self.steps:
            steps[5]()


def gather_steps(src, out, route, send, recv, local, arrived=None, depth=3):
    y, x, c, z = place_of()
    near = [device_of(y, 1 - x, c, z), device_of(1 - y, x, c, z)]
    own, row, plane = out.at[y, x, c], (out.at[:, x, c] if route else out.at[y, :, c]), out.at[:, :, c]
    dst = out.at[y, x, c, z]
    mine = pltpu.make_async_copy(src, dst, local)
    line = [remote(src, dst, send, recv, k, device_of(y, x, c, (z + k + 1) % 4)) for k in range(HOPS)]
    first = Spread(own, own, send, recv, 3, near[route], depth)
    second = Spread(row, row, send, recv, 4, near[1 - route], depth)
    pair = Spread(plane, plane, send, recv, 5, device_of(y, x, 1 - c, z), depth)

    def begin():
        for copy in line + [mine]:
            copy.start()

    def after_line():
        mine.wait()
        for copy in line:
            copy.wait_recv()
        first.start()

    def after_first():
        first.wait_recv()
        second.start()

    def after_second():
        second.wait_recv()
        pair.start()

    def finish():
        pair.wait_recv()
        if arrived is not None:
            arrived()

    def close():
        for copy in line + [first, second, pair]:
            copy.wait_send()

    return [begin, after_line, after_first, after_second, finish, close]


def add_blocks(count, left, right):
    def body(i, carry):
        a = left(i)
        a[...] = a[...] + right(i)[...]
        return carry

    lax.fori_loop(0, count, body, 0)


def scatter_steps(grads, out, route, buffers):
    held, got, mid, last, ends, send, recv, local = buffers
    y, x, c, z = place_of()
    apart = held is not None
    if not apart:
        held = grads.at[:, :, c]
    near = [device_of(1 - y, x, c, z), device_of(y, 1 - x, c, z)]
    mine = pltpu.make_async_copy(grads.at[:, :, c], held, local) if apart else None
    pair = Spread(grads.at[:, :, 1 - c], got, send, recv, 0, device_of(y, x, 1 - c, z), 2)
    first = remote(held.at[:, 1 - x] if route else held.at[1 - y], mid, send, recv, 1, near[route])
    second = remote(held.at[1 - y, x] if route else held.at[y, 1 - x], last, send, recv, 2, near[1 - route])
    line = [
        remote(held.at[y, x, (z + k + 1) % 4], ends.at[k], send, recv, 3 + k, device_of(y, x, c, (z + k + 1) % 4))
        for k in range(HOPS)
    ]

    def begin():
        if apart:
            mine.start()
        pair.start()

    def after_pair():
        if apart:
            mine.wait()
        pair.wait_recv()
        add_blocks(4, lambda i: held.at[i // 2, i % 2], lambda i: got.at[i // 2, i % 2])
        first.start()

    def after_first():
        first.wait_recv()
        if route:
            add_blocks(2, lambda i: held.at[i, x], lambda i: mid.at[i])
        else:
            add_blocks(2, lambda i: held.at[y, i], lambda i: mid.at[i])
        second.start()

    def after_second():
        second.wait_recv()
        add_blocks(1, lambda i: held.at[y, x], lambda i: last)
        for copy in line:
            copy.start()

    def finish():
        for copy in line:
            copy.wait_recv()
        total = held[y, x, z].astype(F32)
        for k in range(HOPS):
            total = total + ends[k].astype(F32)
        out[...] = total

    def close():
        for copy in [pair, first, second] + line:
            copy.wait_send()

    return [begin, after_pair, after_first, after_second, finish, close]


def scatter_buffers(shape, dtype):
    return [
        pltpu.VMEM(lead + shape, dtype) for lead in ((2, 2, 4), (2, 2, 4), (2, 4), (4,), (HOPS,))
    ] + [pltpu.SemaphoreType.DMA((SLOTS,)), pltpu.SemaphoreType.DMA((SLOTS,)), pltpu.SemaphoreType.DMA]


def tile_at(index, width):
    return pl.ds(pl.multiple_of(index * width, width), width)


def fetch(src, dst, sem):
    copy = pltpu.make_async_copy(src, dst, sem)
    copy.start()
    return copy


def no_step():
    pass


def pieces(total, cuts, body, step):
    bounds = [total * i // cuts for i in range(cuts + 1)]
    for low, high in zip(bounds, bounds[1:]):
        lax.fori_loop(low, high, lambda i, c: (body(i), c)[1], 0)
        step()


def rows2d(values):
    return values.reshape(-1, values.shape[-1])


def stream_tiles(tiles, compute, buf_ref, dst_of, sem, step=no_step, cuts=1):
    def copy(n):
        slot = lax.rem(n, 2)
        return pltpu.make_async_copy(buf_ref.at[slot], dst_of(n), sem.at[slot])

    def body(n):
        @pl.when(n >= 2)
        def _():
            copy(n - 2).wait()

        buf_ref[lax.rem(n, 2)] = compute(n)
        copy(n).start()

    pieces(tiles, cuts, body, step)
    for n in range(max(tiles - 2, 0), tiles):
        copy(n).wait()


def transpose_into(src_ref, dst_ref):
    for col in range(0, src_ref.shape[1], 256):
        dst_ref[col : col + 256, :] = src_ref[:, col : col + 256].T


def affine(xhat, gains_ref, row):
    return (xhat * gains_ref[row : row + 1] + gains_ref[row + 1 : row + 2]).astype(BF)


def frame_at(f, count, frames):
    return pl.ds(f, count, frames)


def get_rows(ref, at):
    return jnp.concatenate([ref[j, at, :] for j in range(ref.shape[0])], axis=1)


def set_rows(ref, at, value):
    for j in range(ref.shape[0]):
        ref[j, at, :] = value[:, j * 128 : j * 128 + 128]


def cuts_of(length, unit):
    parts = 3 if length % (3 * unit) == 0 else 1
    return [(length // parts * i, length // parts) for i in range(parts)]


def fetch_chunks(src, dst, sems):
    width = src.shape[2]
    return [fetch(src.at[j], dst.at[:, pl.ds(j * width, width)], sems.at[j]) for j in range(src.shape[0])]


def weight_view(ref):
    if len(ref.shape) == 3:
        return lambda j, n: ref[j, :, tile_at(n, 256)]
    return lambda j, n: rows2d(ref[j, :, :, :, :, :, tile_at(n, 256)].astype(F32)).astype(BF)


def chunk_tile(ref, n):
    per = ref.shape[2] // 256
    j = lax.div(n, per)
    return ref.at[j, :, tile_at(n - j * per, 256)]


def head_cols(h, width):
    return [pl.ds(s * width + h * 128, 128) for s in range(3)]


def forward(fast, frames, *refs):
    if fast:
        (x_hbm, keep_ref, cls_ref, *vec_refs), (sp, so, sm, zp, zo, di, do), refs = refs[:9], refs[9:16], refs[16:]
        gp, gm, gs, gdi, gdo, *refs = refs
    else:
        (x_hbm, keep_ref, cls_ref, small_ref, gp, gm, gs), refs = refs[:7], refs[7:]
    (after_hbm, tpacked_hbm, tprobs_hbm, tmixed_hbm, proj_hbm, kt_hbm, ks_hbm, gains_ref,
     tok_hbm, spacked_hbm, sprobs_hbm, smixed_hbm, tn_hbm, sn_hbm, *refs) = refs
    (x_ref, n_ref, packed_ref, tprobs_ref, mixed_ref, proj_ref, after_ref, kt_ref, ks_ref, off_ref, turn_ref,
     wp_ref, wm_ref, ws_ref, sprobs_ref, tok_ref, io, psem, *refs) = refs
    padded = ks_ref.shape[1]
    rows, width = x_ref.shape
    count = rows // frames
    edge = count // 16 * 16
    cell = frames * PLACES
    groups = rows // cell
    half = HEADS // 2
    load_x = fetch(x_hbm, x_ref, io.at[0])
    clock = Clock()
    loads = {}
    places = [(gp, wp_ref, j) for j in range(3)] + [(gm, wm_ref, j) for j in range(2)] + [(gs, ws_ref, j) for j in range(4)]

    def move(key):
        outside, inside, j = places[key]
        ends = (inside.at[j], outside.at[j]) if fast else (outside.at[j], inside.at[j])
        loads[key] = fetch(*ends, io.at[12 + key])

    if fast:
        small_ref, share_ref, send, recv, local = refs
        share = vec_refs[0].shape[1]
        turn_ref[...] = jnp.zeros_like(turn_ref)
        for i, vec in enumerate(vec_refs):
            turn_ref[i : i + 1, :share] = vec[...].astype(F32)
        share_ref[...] = turn_ref[:, :128].T[:share]
        def columns_of(ref):
            return [ref.at[:, pl.ds(at, width)] for at in range(0, ref.shape[1], width)]

        shards = [c for ref in (sp, so, sm, zp, zo) for c in columns_of(ref)]
        chunks = [(src, w.at[j], functools.partial(move, i)) for i, (src, (_, w, j)) in enumerate(zip(shards, places))]
        chunks += [(src, gdi.at[j], None) for j, src in enumerate(columns_of(di))]
        chunks += [(do.at[pl.ds(a, n)], gdo.at[i], None) for i, (a, n) in enumerate(cuts_of(do.shape[0], 16))]
        meet()
        steps = [
            gather_steps(s, g, i % 2, send.at[i], recv.at[i], local.at[i], done, 3 if done else 2) for i, (s, g, done) in enumerate(chunks)
        ]
        last = len(chunks)
        small = gather_steps(share_ref, small_ref, 0, send.at[last], recv.at[last], local.at[last])
        sizes = [src.shape[0] * width / 512.0 for src, _, _ in chunks]
        clock = Clock([(GATHER[0], share / 2.0, small)] + [(GATHER[i % 2], n, c) for i, (n, c) in enumerate(zip(sizes, steps))], None, 1.35)
        clock.spend(0.0)
    else:
        for key in range(len(places)):
            move(key)

    def need(key):
        clock.need(key + 1)
        if not fast:
            loads[key].wait()

    turn_ref[...] = jnp.zeros_like(turn_ref)
    turn_ref[:frames, :count] = keep_ref[...].astype(F32)
    columns = turn_ref[...].T
    for f in range(frames):
        spread = jnp.broadcast_to(columns[:padded, f : f + 1], (padded, 128))
        ks_ref[f] = spread
        ks_ref[f, count : count + 1, :] = jnp.ones((1, 128), F32)
        kt_ref[frame_at(f, count, frames), :] = spread[:count]
    kt_ref[rows:, :] = jnp.zeros((kt_ref.shape[0] - rows, 128), F32)
    kt_ref[rows : rows + 1, :] = jnp.ones((1, 128), F32)
    clock.spend(1.5)
    across = off_ref.shape[1]
    place = lax.broadcasted_iota(jnp.int32, (cell, across), 0) // frames
    query = lax.broadcasted_iota(jnp.int32, (cell, across), 1)
    query = jnp.where(query < across // 2, query, query - across // 2) // frames
    off_ref[...] = jnp.where(place == query, 0.0, FAR)
    outs = [fetch(kt_ref, kt_hbm, io.at[1]), fetch(ks_ref, ks_hbm, io.at[2])]
    clock.spend(1.0)
    if fast:
        clock.need(0)
        gains_ref[...] = rows2d(small_ref[...]).T[:8]
    else:
        gains_ref[...] = small_ref[...]
    load_x.wait()

    def norm_chunk(i):
        at = tile_at(i, cell)
        xhat, _ = norm_stats(x_ref[at, :].astype(F32))
        n_ref[at, :] = affine(xhat, gains_ref, 0)

    pieces(groups, 2, norm_chunk, lambda: clock.spend(1.5))
    normed_out = fetch(n_ref.at[:rows], tn_hbm, io.at[21])
    get_p, get_m, get_s = weight_view(wp_ref), weight_view(wm_ref), weight_view(ws_ref)

    tiles = width // 256
    for j in range(3):
        need(j)

        def project_tile(n):
            packed_ref[:rows, tile_at(j * tiles + n, 256)] = dot(n_ref[:rows, :], get_p(j, n)).astype(BF)

        pieces(tiles, 1, project_tile, lambda: clock.spend(2.0))
    outs.append(fetch(packed_ref.at[:rows], tpacked_hbm, io.at[4]))

    def group(g):
        at = tile_at(g, cell)
        bias = off_ref[...] + jnp.where(kt_ref[at, 0:1] > 0.5, 0.0, NEG)
        for h in range(half):
            q, k, v = (packed_ref[at, c] for c in head_cols(h, width))
            probs, mixed = attend_unit(q, k, v, bias)
            tprobs_ref[g, h] = probs
            mixed_ref[at, h * 128 : h * 128 + 128] = mixed

    pieces(groups, 7, group, lambda: clock.spend(2.2))
    outs.append(fetch(tprobs_ref, tprobs_hbm, io.at[5]))
    mixed_out = fetch(mixed_ref.at[:rows], tmixed_hbm, io.at[6])
    need(3)
    need(4)

    def output_tile(n):
        cols = tile_at(n, 256)
        proj_ref[:, cols] = dot(mixed_ref[:rows, :], get_m(0, n)).astype(BF)

    pieces(width // 256, 1, output_tile, lambda: clock.spend(2.0))
    outs.append(fetch(proj_ref, proj_hbm, io.at[7]))

    def mixer_tile(n):
        cols = tile_at(n, 256)
        branch = dot(proj_ref[...], get_m(1, n))
        value = x_ref[:, cols].astype(F32) + branch * kt_ref[:rows, 0:1]
        for part in range(2):
            after_ref[2 * n + part] = value[:, part * 128 : part * 128 + 128]

    pieces(width // 256, 1, mixer_tile, lambda: clock.spend(2.5))
    outs.append(fetch(after_ref, after_hbm, io.at[8]))
    normed_out.wait()
    xhat, _ = norm_stats(cls_ref[...].astype(F32))
    class_normed = affine(xhat, gains_ref, 2)
    for f in range(frames):
        xhat, _ = norm_stats(get_rows(after_ref, frame_at(f, count, frames)))
        at = f * padded
        n_ref[at + edge : at + padded, :] = jnp.zeros((padded - edge, width), BF)
        n_ref[at : at + count, :] = affine(xhat, gains_ref, 2)
        n_ref[at + count : at + count + 1, :] = class_normed
    clock.spend(3.0)
    outs.append(fetch(n_ref, sn_hbm, io.at[22]))
    outs.pop(2).wait()

    for j in range(3):
        need(5 + j)

        def space_tile(n):
            packed_ref[:, tile_at(j * tiles + n, 256)] = dot(n_ref[...], get_s(j, n)).astype(BF)

        pieces(tiles, 1, space_tile, lambda: clock.spend(2.0))
    outs.append(fetch(packed_ref, spacked_hbm, io.at[9]))
    mixed_out.wait()

    def probs_out(f):
        slot = lax.rem(f, 2)
        return pltpu.make_async_copy(sprobs_ref.at[slot], sprobs_hbm.at[f], psem.at[slot])

    def frame(f):
        at = tile_at(f, padded)
        bias = jnp.where(ks_ref[f][:, 0:1] > 0.5, 0.0, NEG)

        @pl.when(f >= 2)
        def _():
            probs_out(f - 2).wait()

        for h in range(half):
            q, k, v = (packed_ref[at, c] for c in head_cols(h, width))
            probs, mixed = attend_unit(q, k, v, bias)
            sprobs_ref[lax.rem(f, 2), h] = probs
            mixed_ref[at, h * 128 : h * 128 + 128] = mixed
        probs_out(f).start()

    pieces(frames, 8, frame, lambda: clock.spend(2.2))
    outs.append(fetch(mixed_ref, smixed_hbm, io.at[10]))
    need(8)
    for n in range(width // 256):
        cols = pl.ds(n * 256, 256)
        branch = dot(mixed_ref[...], get_s(3, n))
        total = jnp.zeros((1, 256), F32)
        for f in range(frames):
            part = branch[f * padded : (f + 1) * padded]
            total = total + part[count : count + 1]
            for side in range(2):
                j = 2 * n + side
                at = frame_at(f, count, frames)
                inner = part[:count, side * 128 : side * 128 + 128]
                tok_ref[j, at, :] = after_ref[j, at, :] + inner * ks_ref[f, :count, :]
        row = cls_ref[:, cols].astype(F32) + total * (1.0 / frames)
        for side in range(2):
            tok_ref[2 * n + side, rows:, :] = jnp.zeros((tok_ref.shape[1] - rows, 128), F32)
            tok_ref[2 * n + side, rows : rows + 1, :] = row[:, side * 128 : side * 128 + 128]
    outs.append(fetch(tok_ref, tok_hbm, io.at[11]))
    clock.drain()
    for f in range(frames - 2, frames):
        probs_out(f).wait()
    for copy in outs + (list(loads.values()) if fast else []):
        copy.wait()
    clock.close()


def dense_both(
    parts, tok_hbm, kt_ref, cot_hbm, cotc_ref, gains_ref, wi_hbm, do_hbm,
    pout_hbm, cout_ref, gtok_hbm, dwi_hbm, dwo_hbm, dgb_ref,
    tok_ref, cot_ref, wi_ref, wo_ref, pout_ref, act_ref, gh_ref, dn_ref, gdb_ref, lt_ref,
    pre_a, pre_b, grad_a, grad_b, bi_ref, bo_ref, io, sem, wsem, isem,
):
    total, width = dn_ref.shape
    rows = pout_ref.shape[0]
    hidden = wo_ref.shape[0]
    span, narrow = pre_a.shape
    cell = 112
    load_tok = fetch(tok_hbm, tok_ref, io.at[0])
    load_wi = fetch_chunks(wi_hbm, wi_ref, isem)
    load_cot = fetch(cot_hbm, cot_ref.at[pl.ds(0, rows)], io.at[1])
    cot_ref[rows:, :] = jnp.zeros((total - rows, width), BF)
    cot_ref[rows : rows + 1, :] = cotc_ref[...]
    load_wo = []
    for i in range(parts):
        for b in range(do_hbm.shape[0] // parts):
            n = do_hbm.shape[1]
            load_wo.append(fetch(do_hbm.at[i * (do_hbm.shape[0] // parts) + b], wo_ref.at[pl.ds((b * parts + i) * n, n)], wsem.at[i, b]))
    dgb_ref[...] = jnp.zeros_like(dgb_ref)
    load_tok.wait()
    load_cot.wait()

    def first_rows(i):
        at = tile_at(i, cell)
        gdb_ref[at, :] = (cot_ref[at, :].astype(F32) * kt_ref[at, 0:1]).astype(BF)
        xhat, _ = norm_stats(get_rows(tok_ref, at))
        dn_ref[at, :] = affine(xhat, gains_ref, 4)

    pieces(rows // cell, 1, first_rows, no_step)
    xhat, _ = norm_stats(get_rows(tok_ref, pl.ds(rows, total - rows)))
    dn_ref[rows:, :] = affine(xhat, gains_ref, 4)
    gdb_ref[rows:, :] = cot_ref[rows:, :]
    for copy in load_wi + load_wo:
        copy.wait()
    across = hidden // narrow
    count = total // span * across

    def spot(i):
        r = i // across if isinstance(i, int) else lax.div(i, across)
        return tile_at(r, span), i - r * across

    def multiply(i, pre_ref, grad_ref):
        at, n = spot(i)
        pre_ref[...] = dot(dn_ref[at, :], wi_ref[:, tile_at(n, narrow)])
        grad_ref[...] = dot(gdb_ref[at, :], wo_ref[tile_at(n, narrow), :], NT)

    def activate(i, pre_ref, grad_ref):
        at, n = spot(i)
        cols = tile_at(n, narrow)
        act, slope = gelu_pair(pre_ref[...])
        act_ref[at, cols] = act.astype(BF)
        gh_ref[at, cols] = (slope * grad_ref[...]).astype(BF)

    multiply(0, pre_a, grad_a)

    def two(j):
        multiply(2 * j + 1, pre_b, grad_b)
        activate(2 * j, pre_a, grad_a)
        multiply(2 * j + 2, pre_a, grad_a)
        activate(2 * j + 1, pre_b, grad_b)

    pieces(count // 2 - 1, 1, two, no_step)
    multiply(count - 1, pre_b, grad_b)
    activate(count - 2, pre_a, grad_a)
    activate(count - 1, pre_b, grad_b)

    def branch_tile(n):
        cols = tile_at(n, 256)
        branch = dot(act_ref[...], wo_ref[:, cols])
        result = jnp.concatenate([tok_ref[2 * n], tok_ref[2 * n + 1]], axis=1) + branch * kt_ref[:, 0:1]
        pout_ref[:, cols] = result[:rows].astype(BF)
        cout_ref[:, cols] = result[rows : rows + 1].astype(BF)

    pieces(width // 256, 1, branch_tile, no_step)
    out_p = fetch(pout_ref, pout_hbm, io.at[4])

    def back(r):
        base = r * span
        grad_normed = dot(gh_ref[tile_at(r, span), :], wi_ref[...], NT)
        for part in range(span // 48):
            at = pl.ds(pl.multiple_of(base + part * 48, 16), 48)
            grad = grad_normed[part * 48 : part * 48 + 48]
            xhat, scale = norm_stats(get_rows(tok_ref, at))
            dgb_ref[0] += fold8(grad * xhat)
            dgb_ref[1] += fold8(grad)
            set_rows(tok_ref, at, norm_back(xhat, scale, gains_ref[4:5], grad) + cot_ref[at, :].astype(F32))

    pieces(total // span, 1, back, no_step)

    out_t = fetch(tok_ref, gtok_hbm, io.at[5])
    transpose_into(dn_ref, lt_ref)

    def in_tile(n):
        return dot(lt_ref[...], gh_ref[:, tile_at(n, 256)]).astype(BF)

    stream_tiles(hidden // 256, in_tile, bi_ref, lambda n: chunk_tile(dwi_hbm, n), sem)
    transpose_into(gdb_ref, lt_ref)

    def out_tile(n):
        return dot(lt_ref[...], act_ref[:, tile_at(n, 256)]).T.astype(BF)

    stream_tiles(hidden // 256, out_tile, bo_ref, lambda n: dwo_hbm.at[tile_at(n, 256), :], sem)
    out_p.wait()
    out_t.wait()


def space_backward(fast, *refs):
    gtok_hbm, after_hbm, cls_ref, ks_ref, gains_ref, w_hbm, packed_hbm, probs_hbm, mixed_hbm, sn_hbm, *refs = refs
    if fast:
        dwi_hbm, dwo_hbm, *refs = refs
    gafter_hbm, gcls_ref, dw_hbm, dgb_ref, *refs = refs
    if fast:
        di_ref, do_ref, *refs = refs
    gtok_ref, after_ref, w_ref, packed_ref, gsb_ref, gm_ref, lt_ref, pbuf_ref, tile_ref, io, sem, psem, isem, *refs = refs
    frames, padded = ks_ref.shape[:2]
    rows, width = after_ref.shape[1], w_ref.shape[0]
    count = rows // frames
    edge = count // 16 * 16

    def load(f):
        slot = lax.rem(f, 2)
        return pltpu.make_async_copy(probs_hbm.at[f], pbuf_ref.at[slot], psem.at[slot])

    load_gtok = fetch(gtok_hbm, gtok_ref, io.at[0])
    load_w = fetch_chunks(w_hbm, w_ref, isem)
    load_packed = fetch(packed_hbm, packed_ref, io.at[2])
    load(0).start()
    load_after = fetch(after_hbm, after_ref, io.at[3])
    clock = Clock()
    if fast:
        meet()
        pairs = [(dwi_hbm.at[j], di_ref.at[:, pl.ds(j * width, width)]) for j in range(dwi_hbm.shape[0])]
        pairs += [(dwo_hbm.at[:, :, :, :, pl.ds(a, n)], do_ref.at[pl.ds(a, n)]) for a, n in cuts_of(do_ref.shape[0], 16)]
        clock = Clock([
            (SCATTER[i % 2], o.shape[0] * o.shape[1] / 512.0, scatter_steps(g, o, i % 2, refs[8 * i : 8 * i + 8]))
            for i, (g, o) in enumerate(pairs)
        ])
        clock.spend(0.0)
    dgb_ref[...] = jnp.zeros_like(dgb_ref)
    load_gtok.wait()
    class_grad = get_rows(gtok_ref, pl.ds(rows, 1))
    for f in range(frames):
        at = f * padded
        gsb_ref[at + edge : at + padded, :] = jnp.zeros((padded - edge, width), BF)
        grad = get_rows(gtok_ref, frame_at(f, count, frames)) * ks_ref[f, :count, 0:1]
        gsb_ref[at : at + count, :] = grad.astype(BF)
        gsb_ref[at + count : at + count + 1, :] = (class_grad * (1.0 / frames)).astype(BF)
    clock.spend(3.5)
    for copy in load_w:
        copy.wait()

    def back_tile(n):
        at = tile_at(n, 256)
        gm_ref[:, at] = dot(gsb_ref[...], w_ref[at, 3 * width :], NT).astype(BF)

    pieces(width // 256, 1, back_tile, lambda: clock.spend(2.0))
    load_packed.wait()

    def frame(f):
        at = tile_at(f, padded)
        load(f).wait()

        @pl.when(f + 1 < frames)
        def _():
            load(f + 1).start()

        for h in range(HEADS // 2):
            cols = head_cols(h, width)
            q, k, v = (packed_ref[at, c] for c in cols)
            grads = attend_unit_back(q, k, v, pbuf_ref[lax.rem(f, 2), h], gm_ref[at, cols[0]])
            for c, grad in zip(cols, grads):
                packed_ref[at, c] = grad

    pieces(frames, 8, frame, lambda: clock.spend(3.0))
    load_mixed = fetch(mixed_hbm, gm_ref, io.at[4])
    load_after.wait()
    load_mixed.wait()
    transpose_into(gm_ref, lt_ref)
    load_normed = fetch(sn_hbm, gm_ref, io.at[1])

    def out_tile(n):
        return dot(lt_ref[...], gsb_ref[:, tile_at(n, 256)]).astype(BF)

    stream_tiles(width // 256, out_tile, tile_ref, lambda n: dw_hbm.at[3, :, tile_at(n, 256)], sem)
    clock.spend(3.0)
    xhat_class, scale_class = norm_stats(cls_ref[...].astype(F32))
    load_normed.wait()
    transpose_into(gm_ref, lt_ref)

    def in_tile(n):
        return dot(lt_ref[...], packed_ref[:, tile_at(n, 256)]).astype(BF)

    stream_tiles(3 * width // 256, in_tile, tile_ref, lambda n: chunk_tile(dw_hbm, n), sem, lambda: clock.spend(3.0), 3)
    gcls_ref[...] = class_grad
    whole = count // 8 * 8
    for i in range(0, frames, 2):
        grad_normed = dot(packed_ref[i * padded : (i + 2) * padded, :], w_ref[:, : 3 * width], NT)
        for j in range(2):
            grad = grad_normed[j * padded : j * padded + count]
            class_row = grad_normed[j * padded + count : j * padded + count + 1]
            at = frame_at(i + j, count, frames)
            xhat, scale = norm_stats(get_rows(after_ref, at))
            dgb_ref[0] += fold8(grad[:whole] * xhat[:whole])
            dgb_ref[1] += fold8(grad[:whole])
            rest = grad[whole:]
            dgb_ref[0, 0:1, :] += jnp.sum(rest * xhat[whole:], axis=0, keepdims=True) + class_row * xhat_class
            dgb_ref[1, 0:1, :] += jnp.sum(rest, axis=0, keepdims=True) + class_row
            set_rows(gtok_ref, at, get_rows(gtok_ref, at) + norm_back(xhat, scale, gains_ref[2:3], grad))
            gcls_ref[...] += norm_back(xhat_class, scale_class, gains_ref[2:3], class_row)
        clock.spend(3.0)
    out = fetch(gtok_ref.at[:, :rows], gafter_hbm, io.at[5])
    clock.drain()
    out.wait()
    clock.close()


def time_backward(fast, *refs):
    gafter_hbm, x_hbm, kt_ref, gains_ref, wp_hbm, wm_hbm, packed_hbm, probs_hbm, mixed_hbm, proj_hbm, xn_hbm, *refs = refs
    if fast:
        dws_hbm, dspace_ref, ddense_ref, *refs = refs
        gx_hbm, ds_ref, dm_ref, dp_ref, dsmall_ref, *refs = refs
    else:
        gx_hbm, dgb_ref, *refs = refs
    (gafter_ref, x_ref, wp_ref, wm_ref, packed_ref, pbuf_ref, mixed_ref, proj_ref, gtb_ref, gproj_ref, gm_ref, lt_ref,
     dwm_ref, dwp_ref, io, psem, isem, *refs) = refs
    rows, width = x_ref.shape
    cell = pbuf_ref.shape[2]
    groups = rows // cell
    load_gafter = fetch(gafter_hbm, gafter_ref, io.at[0])
    load_wm = fetch(wm_hbm, wm_ref, io.at[1])
    load_proj = fetch(proj_hbm, proj_ref, io.at[2])
    load_mixed = fetch(mixed_hbm, mixed_ref, io.at[3])
    load_packed = fetch(packed_hbm, packed_ref, io.at[4])
    load_x = fetch(x_hbm, x_ref, io.at[5])
    load_wp = fetch_chunks(wp_hbm, wp_ref, isem)

    def load(g):
        slot = lax.rem(g, 2)
        return pltpu.make_async_copy(probs_hbm.at[g], pbuf_ref.at[slot], psem.at[slot])

    load(0).start()
    clock = Clock()
    if fast:
        dgb_ref, turn_ref, gsmall_ref, *refs = refs
        meet()
        space = [
            scatter_steps(dws_hbm.at[j], ds_ref.at[:, pl.ds(j * width, width)], j % 2, refs[8 * j : 8 * j + 8])
            for j in range(dws_hbm.shape[0])
        ]
        refs = refs[8 * len(space) :]

        def part_steps(grad_ref, out_ref, j, route, buffers):
            return scatter_steps(grad_ref.at[j], out_ref.at[:, pl.ds(j * width, width)], route, [None] + buffers)

        mixer = [part_steps(dwm_ref, dm_ref, j, j, refs[7 * j : 7 * j + 7]) for j in range(2)]
        project = [part_steps(dwp_ref, dp_ref, j, j % 2, refs[14 + 7 * j : 21 + 7 * j]) for j in range(3)]
        small = scatter_steps(gsmall_ref, dsmall_ref, 1, [None] + refs[35:])
        size = ds_ref.shape[0] * width / 512.0
        known = [(SCATTER[j % 2], size, c) for j, c in enumerate(space)]
        known += [(SCATTER[r], size, c) for r, c in ((1, mixer[1]), (0, mixer[0]), (0, project[0]), (1, project[1]), (0, project[2]))]
        known.append((SCATTER[1], ds_ref.shape[0] / 2.0, small))
        clock = Clock(known, [None] * len(space) + [13.0, 16.0, 42.5, 45.5, 48.5, 60.0])
        clock.spend(0.0)

    def begin(chunk):
        if fast:
            clock.need(len(space) + chunk, 0)

    def put(ref, j, n, value):
        cols = tile_at(n, 256)
        if len(ref.shape) == 3:
            ref[j, :, cols] = value.astype(BF)
        else:
            ref[j, :, :, :, :, :, cols] = value.reshape(ref.shape[1:6] + (256,)).astype(BF)

    dgb_ref[...] = jnp.zeros_like(dgb_ref)
    load_gafter.wait()

    def branch_rows(i):
        at = tile_at(i, cell)
        gtb_ref[at, :] = (get_rows(gafter_ref, at) * kt_ref[at, 0:1]).astype(BF)

    pieces(groups, 1, branch_rows, no_step)
    load_wm.wait()

    def back_mixer(n):
        at = tile_at(n, 256)
        gproj_ref[:, at] = dot(gtb_ref[...], wm_ref[1, at, :], NT).astype(BF)

    def back_output(n):
        at = tile_at(n, 256)
        gm_ref[:, at] = dot(gproj_ref[...], wm_ref[0, at, :], NT).astype(BF)

    pieces(width // 256, 1, back_mixer, no_step)
    pieces(width // 256, 1, back_output, no_step)
    clock.spend(8.0)
    load_proj.wait()
    transpose_into(proj_ref, lt_ref)
    tiles = width // 256
    pieces(tiles, 1, lambda n: put(dwm_ref, 1, n, dot(lt_ref[...], gtb_ref[:, tile_at(n, 256)])), no_step)
    load_normed = fetch(xn_hbm, gtb_ref, io.at[6])
    clock.spend(3.0)
    begin(0)
    load_mixed.wait()
    transpose_into(mixed_ref, lt_ref)
    pieces(tiles, 1, lambda n: put(dwm_ref, 0, n, dot(lt_ref[...], gproj_ref[:, tile_at(n, 256)])), no_step)
    clock.spend(2.9)
    begin(1)
    load_packed.wait()

    def group(g):
        at = tile_at(g, cell)
        load(g).wait()

        @pl.when(g + 1 < groups)
        def _():
            load(g + 1).start()

        for h in range(HEADS // 2):
            cols = head_cols(h, width)
            q, k, v = (packed_ref[at, c] for c in cols)
            grads = attend_unit_back(q, k, v, pbuf_ref[lax.rem(g, 2), h], gm_ref[at, h * 128 : h * 128 + 128])
            for c, grad in zip(cols, grads):
                packed_ref[at, c] = grad

    pieces(groups, 7, group, lambda: clock.spend(3.2))
    load_x.wait()
    load_normed.wait()
    transpose_into(gtb_ref, lt_ref)
    for j in range(3):
        pieces(tiles, 1, lambda n: put(dwp_ref, j, n, dot(lt_ref[...], packed_ref[:, tile_at(j * tiles + n, 256)])), no_step)
        clock.spend(2.7)
        begin(2 + j)
    for copy in load_wp:
        copy.wait()
    span = rows // 2

    def back(r):
        grad_normed = dot(packed_ref[tile_at(r, span), :], wp_ref[...], NT)
        for part in range(span // cell):
            at = pl.ds(r * span + part * cell, cell)
            grad = grad_normed[part * cell : part * cell + cell]
            xhat, scale = norm_stats(x_ref[at, :].astype(F32))
            dgb_ref[0] += fold8(grad * xhat)
            dgb_ref[1] += fold8(grad)
            out = norm_back(xhat, scale, gains_ref[0:1], grad)
            x_ref[at, :] = (get_rows(gafter_ref, at) + out).astype(BF)
            clock.spend(0.75)

    for r in range(rows // span):
        back(r)
    out = fetch(x_ref, gx_hbm, io.at[7])
    if fast:
        turn_ref[...] = jnp.zeros_like(turn_ref)
        for i, ref in enumerate((dgb_ref, dspace_ref, ddense_ref)):
            for j in range(2):
                turn_ref[2 * i + j : 2 * i + j + 1, :] = jnp.sum(ref[j], axis=0, keepdims=True)
        gsmall_ref[...] = turn_ref[...].T.reshape(gsmall_ref.shape)
        begin(5)
        clock.drain()
        clock.close()
    out.wait()


def finish_all(di, do, ds, dm, dp, dsmall, gcls, gx, *refs):
    odi, odo, osp, oso, otp, oto, otm, ocls, ogx, *vecs = refs[:15]
    turn_ref = refs[15]
    width = oso.shape[1]
    ogx[...] = gx[...]
    odi[...] = di[...]
    odo[...] = do[...]
    osp[...] = ds[:, : 3 * width]
    oso[...] = ds[:, 3 * width :]
    otp[...] = dp[...]
    oto[...] = dm[:, :width]
    otm[...] = dm[:, width:]
    ocls[...] = gcls[...].astype(BF)
    share = dsmall.shape[0]
    turn_ref[...] = jnp.zeros_like(turn_ref)
    turn_ref[:share, :] = dsmall[...]
    turned = turn_ref[...].T
    for i, vec in enumerate(vecs):
        vec[...] = turned[i : i + 1, :share]


VM = pl.BlockSpec(memory_space=pltpu.VMEM)
ANY = pl.BlockSpec(memory_space=pl.ANY)


def call(kernel, args, outs, scratch, flops=0, remote_id=None):
    params = {}
    if remote_id is not None:
        params = {"collective_id": remote_id, "has_side_effects": True}
    return pl.pallas_call(
        kernel,
        out_shape=[jax.ShapeDtypeStruct(*o[0]) for o in outs],
        in_specs=[a[1] for a in args],
        out_specs=[o[1] for o in outs],
        scratch_shapes=scratch,
        compiler_params=pltpu.CompilerParams(vmem_limit_bytes=LIMIT, **params),
        cost_estimate=pl.CostEstimate(flops=flops, bytes_accessed=40 * 2**20, transcendentals=0),
    )(*[a[0] for a in args])


def gather(value):
    return lax.all_gather(value, AXES, axis=0, tiled=True)


def scatter(value):
    return lax.psum_scatter(value, AXES, scatter_dimension=0, tiled=True)


def per_device(
    fast, patches, class_token, keep_mask,
    time_gain, time_bias, time_project, time_output, time_mixer,
    space_gain, space_bias, space_project, space_output,
    dense_gain, dense_bias, dense_in, dense_out,
    cotangent_patches, cotangent_class,
):
    _, frames, count, width = patches.shape
    hidden = dense_in.shape[1]
    share = time_gain.shape[0]
    padded = -(-(count + 1) // 16) * 16
    rows, total, stacked = count * frames, count * frames + 16, frames * padded
    slabs = width // 128
    slab_rows, slab_total = ((slabs, rows, 128), F32), ((slabs, total, 128), F32)
    half = HEADS // 2
    cell = frames * PLACES
    groups = rows // cell
    wide = 3 * width
    dma = pltpu.SemaphoreType.DMA
    vmem = pltpu.VMEM
    devices = (2, 2, 2, 4)

    def by_place(a):
        return jnp.transpose(a[0], (1, 0, 2)).reshape(rows, width)

    def by_frame(a):
        return jnp.transpose(a.reshape(count, frames, width), (1, 0, 2))[None]

    x = by_place(patches)
    vectors = (time_gain, time_bias, space_gain, space_bias, dense_gain, dense_bias)
    flat = ((rows, width), BF)
    deep = ((stacked, width), BF)
    tprobs = (groups, half, cell, 2 * (cell + -cell % 128))
    sprobs = (frames, half, padded, 2 * (padded + -padded % 128))
    parts = hidden // width
    cuts = cuts_of(dense_out.shape[0], 16) if fast else [(0, hidden)]
    blocks = {n: ((n,) + devices + (share, width), BF) for n in (2, 3, 4, parts)}
    chunks = {n: ((n, width, width), BF) for n in (2, 3, 4, parts)}

    def by_chunk(w):
        return jnp.transpose(w.reshape(width, -1, width), (1, 0, 2))

    def by_row(w):
        return jnp.transpose(w, (1, 0, 2)).reshape(width, -1)

    if fast:
        args = [(x, ANY), (keep_mask[0], VM), (class_token, VM)] + [(v.reshape(1, share), VM) for v in vectors]
        args += [(w, VM) for w in (time_project, time_output, time_mixer, space_project, space_output, dense_in, dense_out)]
        outs = [(blocks[n], ANY) for n in (3, 2, 4, parts)]
        outs += [(((len(cuts),) + devices + (cuts[0][1], width), BF), ANY)]
        weights = [vmem(*blocks[n]) for n in (3, 2, 4)]
        comm = [vmem(devices + (share, 128), F32), vmem((share, 128), F32), dma((13 + parts, SLOTS)), dma((13 + parts, SLOTS)), dma((13 + parts,))]
    else:
        small = gather(jnp.stack(vectors, axis=1).astype(F32)).T
        wtp = by_chunk(gather(time_project))
        wtm = by_chunk(gather(jnp.concatenate([time_output, time_mixer], axis=1)))
        wsp = by_chunk(gather(jnp.concatenate([space_project, space_output], axis=1)))
        wdi, wdo = by_chunk(gather(dense_in)), gather(dense_out)[None]
        args = [(x, ANY), (keep_mask[0], VM), (class_token, VM), (jnp.pad(small, ((0, 2), (0, 0))), VM), (wtp, ANY),
                (wtm, ANY), (wsp, ANY)]
        outs, comm = [], []
        weights = [vmem(*chunks[n]) for n in (3, 2, 4)]
    outs += [
        (slab_rows, ANY), (((rows, wide), BF), ANY), ((tprobs, BF), ANY), (flat, ANY), (flat, ANY),
        (((total, 128), F32), ANY), (((frames, padded, 128), F32), ANY), (((8, width), F32), VM),
        (slab_total, ANY), (((stacked, wide), BF), ANY), ((sprobs, BF), ANY), (deep, ANY), (flat, ANY), (deep, ANY),
    ]
    *gathered, after, tpacked, tp, tmixed, tproj, kt, ks, gains, tok, spacked, sp, smixed, tn, sn = call(
        functools.partial(forward, fast, frames), args, outs,
        [vmem(*flat), vmem(*deep), vmem((stacked, wide), BF), vmem(tprobs, BF), vmem(*deep), vmem(*flat),
         vmem(*slab_rows), vmem((total, 128), F32), vmem((frames, padded, 128), F32),
         vmem((cell, tprobs[3]), F32), vmem((128, 256), F32)] + weights
        + [vmem((2,) + sprobs[1:], BF), vmem(*slab_total), dma((23,)), dma((2,))] + comm,
        24 * 10**9, 0 if fast else None,
    )
    if fast:
        wtp, wtm, wsp, wdi = (w.reshape(-1, width, width) for w in gathered[:4])
        wdo = gathered[4].reshape(-1, cuts[0][1], width)

    span = total // 3
    pout, cout, gtok, dwi, dwo, ddense = call(
        functools.partial(dense_both, len(cuts)),
        [(tok, ANY), (kt, VM), (by_place(cotangent_patches), ANY), (cotangent_class, VM), (gains, VM), (wdi, ANY), (wdo, ANY)],
        [(flat, ANY), (((1, width), BF), VM), (slab_total, ANY), (chunks[parts], ANY), (((hidden, width), BF), ANY),
         (((2, 8, width), F32), VM)],
        [vmem(*slab_total), vmem((total, width), BF), vmem((width, hidden), BF), vmem((hidden, width), BF), vmem(*flat),
         vmem((total, hidden), BF), vmem((total, hidden), BF), vmem((total, width), BF), vmem((total, width), BF),
         vmem((width, total), BF)] + [vmem((span, 512), F32)] * 4
        + [vmem((2, width, 256), BF), vmem((2, 256, width), BF), dma((6,)), dma((2,)), dma((len(cuts), 32)), dma((parts,))],
        48 * 10**9,
    )

    args = [(gtok, ANY), (after, ANY), (class_token, VM), (ks, VM), (gains, VM), (wsp, ANY), (spacked, ANY), (sp, ANY),
            (smixed, ANY), (sn, ANY)]
    outs = [(slab_rows, ANY), (((1, width), F32), VM), (chunks[4], ANY),
            (((2, 8, width), F32), VM)]
    comm = []
    if fast:
        args += [(dwi.reshape(blocks[parts][0]), ANY), (dwo.reshape(devices + dense_out.shape), ANY)]
        outs += [((dense_in.shape, F32), VM), ((dense_out.shape, F32), VM)]
        shapes = [(share, width)] * parts + [(n, width) for _, n in cuts]
        comm = [b for s in shapes for b in scatter_buffers(s, BF)]
    gafter, gcls, dws, dspace, *dense_shards = call(
        functools.partial(space_backward, fast), args, outs,
        [vmem(*slab_total), vmem(*slab_rows), vmem((width, 4 * width), BF), vmem((stacked, wide), BF),
         vmem(*deep), vmem(*deep), vmem((width, stacked), BF), vmem((2,) + sprobs[1:], BF), vmem((2, width, 256), BF),
         dma((6,)), dma((2,)), dma((2,)), dma((4,))] + comm,
        20 * 10**9, 2 if fast else None,
    )

    args = [(gafter, ANY), (x, ANY), (kt, VM), (gains, VM), (wtp, ANY), (wtm, ANY), (tpacked, ANY), (tp, ANY),
            (tmixed, ANY), (tproj, ANY), (tn, ANY)]
    scratch = [
        vmem(*slab_rows), vmem(*flat), vmem((width, wide), BF), vmem(*chunks[2]), vmem((rows, wide), BF),
        vmem((2,) + tprobs[1:], BF), vmem(*flat), vmem(*flat), vmem(*flat), vmem(*flat), vmem(*flat), vmem((width, rows), BF),
    ]
    if fast:
        shapes = [(share, n) for n in (4 * width, 2 * width, wide)] + [(share, 128)]
        args += [(dws.reshape(blocks[4][0]), ANY), (dspace, VM), (ddense, VM)]
        gx, ds, dm, dp, dsmall = call(
            functools.partial(time_backward, fast), args, [(flat, ANY)] + [((s, F32), VM) for s in shapes],
            scratch + [vmem(*blocks[2]), vmem(*blocks[3]), dma((8,)), dma((2,)), dma((3,)), vmem((2, 8, width), F32),
                       vmem((128, width), F32), vmem(devices + shapes[3], F32)]
            + scatter_buffers((share, width), BF) * 4 + scatter_buffers((share, width), BF)[1:] * 5 + scatter_buffers(shapes[3], F32)[1:],
            24 * 10**9, 3,
        )
    else:
        def plain(*refs):
            time_backward(False, *refs[:12], refs[14], *refs[15:27], refs[13], refs[12], *refs[27:])

        gx, dp, dm, dtime = call(
            plain, args, [(flat, ANY), (chunks[3], VM), (chunks[2], VM), (((2, 8, width), F32), VM)],
            scratch + [dma((8,)), dma((2,)), dma((3,))], 24 * 10**9,
        )
        dense_shards = [scatter(d).astype(F32) for d in (by_row(dwi), dwo)]
        ds, dm, dp = (scatter(by_row(d)).astype(F32) for d in (dws, dm, dp))
        dsmall = jnp.concatenate([jnp.sum(d, axis=1) for d in (dtime, dspace, ddense)], axis=0)
        vecs = scatter(dsmall.T).T
        shards = (*dense_shards, ds[:, :wide], ds[:, wide:], dp, dm[:, :width], dm[:, width:], gcls.astype(BF), gx)
    if fast:
        shard = [dense_in.shape, dense_out.shape, (share, wide), (share, width), (share, wide), (share, width), (share, width)]
        shards = call(
            finish_all,
            [(a, VM) for a in (*dense_shards, ds, dm, dp, dsmall, gcls, gx)],
            [((s, F32), VM) for s in shard] + [(((1, width), BF), VM), (flat, VM)] + [(((1, share), F32), VM)] * 6,
            [vmem((128, 128), F32)],
        )
        vecs = [v.reshape(share) for v in shards[9:]]
    return (
        by_frame(pout), cout, by_frame(shards[8]), shards[7],
        vecs[0], vecs[1], shards[4], shards[5], shards[6],
        vecs[2], vecs[3], shards[2], shards[3],
        vecs[4], vecs[5], shards[0], shards[1],
    )


def solution(mesh):
    ranks = (4, 2, 3, 1, 1, 2, 2, 2, 1, 1, 2, 2, 1, 1, 2, 2, 4, 2)
    out_ranks = (4, 2, 4, 2, 1, 1, 2, 2, 2, 1, 1, 2, 2, 1, 1, 2, 2)
    fast = mesh.shape["dp"] == 8 and mesh.shape["fsdp"] == 4

    def spec(rank):
        return P(AXES, *([None] * (rank - 1)))

    return jax.shard_map(
        functools.partial(per_device, fast),
        mesh=mesh,
        in_specs=tuple(spec(r) for r in ranks),
        out_specs=tuple(spec(r) for r in out_ranks),
        check_vma=False,
    )
```
